128 devices in a mesh: hi: 4 (over z_lo, core), lo: 32 (over x, y, z_hi).
Axes of the slice: x: 4, y: 4, z: 4 (z_hi: 2, z_lo: 2; z = z_hi * 2 + z_lo), core: 2. Of those that a mesh axis runs over, the one named last changes fastest.
Arguments:
- blocks: bfloat16 [8192, 128, 128], P(('hi', 'lo')), may hold values from -6 to 6
- diag_factors: bfloat16 [4, 8192, 128, 128], P(None, ('hi', 'lo')), may hold values from -0.375 to 0.375
- off_factors: bfloat16 [4, 8192, 128, 128], P(None, ('hi', 'lo')), may hold values from -0.375 to 0.375
- partner_maps: int32 [4, 64], replicated, may hold values from 0 to 63, each once within a row
Outputs:
- summed: bfloat16 [2048, 128, 128], P(('lo', 'hi'))
The draws below stay inside these ranges and needn't reach their ends.
Inputs may be any that keep to these rules, and one draw needn't show every extreme that they name: Each row of partner_maps is a permutation of 0 to 63.
All inputs are finite; a program needn't handle non-finite values.
Results may differ from the reference program's by a relative error of at most 0.009.
Values may be sent and summed in bfloat16 or wider, within the bound.
No kernel may reach another device: no remote copies, remote signals or barrier semaphores. Data moves between devices by JAX's collectives and lax.ppermute only.
A program may use at most 128 MiB of HBM per device.

```python
import jax
import jax.numpy as jnp
import numpy as np

P_SIZE = 128
R = 128
LEVELS = 4
BLK_DEV = 64
NBLK = 8192
N_HI = 4
N_LO = 32


def levels(own_key, extent, cuts, smallest, largest):
    def one(position, shards_of):
        steps = jax.random.uniform(jax.random.fold_in(jax.random.fold_in(own_key, 6), position), (shards_of,), jnp.float32, smallest / len(cuts), largest / len(cuts))
        return jnp.repeat(jnp.exp(steps), extent[position] // shards_of).reshape((-1,) + (1,) * (len(extent) - position - 1))

    loudness = one(*cuts[0])
    for cut in cuts[1:]:
        loudness = loudness * one(*cut)
    return loudness


def noise(stream_key, extent, spread, reach, split=(), held_as=jnp.bfloat16):
    gain = levels(stream_key, extent, split, -0.22, 0.18) if split else 1.0
    array = jax.random.normal(stream_key, extent, jnp.float32) * spread * gain
    return jnp.minimum(jnp.maximum(array, -reach), reach).astype(held_as)


def setup_inputs(seed: int = 0) -> dict:
    seeds = jax.random.split(jax.random.key(seed), 5)
    blocks = noise(seeds[0], (NBLK, R, P_SIZE), 1.0, 6.0, ((0, 128),))
    diag_factors = noise(seeds[1], (LEVELS, NBLK, P_SIZE, P_SIZE), (2 * P_SIZE) ** -0.5, 0.375, ((1, 128),))
    off_factors = noise(seeds[2], (LEVELS, NBLK, P_SIZE, P_SIZE), (2 * P_SIZE) ** -0.5, 0.375, ((1, 128),))
    partner_maps = jax.vmap(lambda own: jax.random.permutation(own, BLK_DEV))(jax.random.split(seeds[3], LEVELS)).reshape((LEVELS, BLK_DEV)).astype(jnp.int32)
    return {"blocks": blocks, "diag_factors": diag_factors, "off_factors": off_factors, "partner_maps": partner_maps}


def apply_factor(factor, data):
    return jnp.einsum("hlbij,hlbrj->hlbri", factor.astype(jnp.float32), data.astype(jnp.float32))


def reference(blocks, diag_factors, off_factors, partner_maps):
    current = blocks.reshape(N_HI, N_LO, BLK_DEV, R, P_SIZE)
    top = N_LO.bit_length() - 1
    for level, bit in enumerate((0, 1, top - 1)):
        order = np.arange(N_LO) ^ (1 << bit)
        partner = current[:, order]
        partner = jnp.take(partner, partner_maps[level].astype(jnp.int32), axis=2)
        diag = diag_factors[level].reshape(N_HI, N_LO, BLK_DEV, P_SIZE, P_SIZE)
        off = off_factors[level].reshape(N_HI, N_LO, BLK_DEV, P_SIZE, P_SIZE)
        mixed = apply_factor(diag, current) + apply_factor(off, partner)
        current = mixed.astype(jnp.bfloat16)
    own = apply_factor(diag_factors[3].reshape(N_HI, N_LO, BLK_DEV, P_SIZE, P_SIZE), current)
    moved = apply_factor(off_factors[3].reshape(N_HI, N_LO, BLK_DEV, P_SIZE, P_SIZE), current)
    order = np.arange(N_HI) ^ 2
    moved = jnp.take(moved[order], partner_maps[3].astype(jnp.int32), axis=2)
    total = jnp.sum(own + moved, axis=0)
    return total.reshape(N_LO * BLK_DEV, R, P_SIZE).astype(jnp.bfloat16)
```

```python
import functools

import jax
import jax.numpy as jnp
from jax import lax
from jax.experimental import pallas as pl
from jax.experimental.pallas import tpu as pltpu
from jax.sharding import PartitionSpec as P

BF = jnp.bfloat16
F32 = jnp.float32
VM = pl.BlockSpec(memory_space=pltpu.VMEM)
SM = pl.BlockSpec(memory_space=pltpu.SMEM)
ANY = pl.BlockSpec(memory_space=pl.ANY)
NB = 64
P_ = 128
PIECES = ((0, 64, (21, 22, 21)), (64, 64, (21, 22, 21)))
DEPTH = 2
CYC, NXT, ST, SRC, TJ, POS, PM3 = range(7)


def partner_2(array, axis, apart):
    return lax.ppermute(array, axis, [(i, i ^ 1 << apart) for i in range(lax.axis_size(axis))])


def mm(left, right):
    return lax.dot_general(left, right, (((1,), (1,)), ((), ())), preferred_element_type=F32)


def cat(a, b):
    return jnp.concatenate([a, b], axis=1)


def call(kernel, name, outs, ins, specs, dep, scratch=(), mb=4, out_specs=None, cost=2000000):
    outs = tuple(outs)
    extra = tuple(dep)

    def run(*refs):
        refs = list(refs)
        n = len(ins)
        del refs[n : n + len(extra)]
        kernel(*refs)

    return pl.pallas_call(
        run,
        out_shape=outs,
        in_specs=list(specs) + [ANY] * len(extra),
        out_specs=tuple(out_specs or [VM] * len(outs)),
        scratch_shapes=list(scratch),
        compiler_params=pltpu.CompilerParams(vmem_limit_bytes=mb << 20),
        cost_estimate=pl.CostEstimate(flops=0, bytes_accessed=cost, transcendentals=0),
        name=name,
    )(*ins, *extra)


def bounds(sizes):
    edge = [0]
    for size in sizes:
        edge.append(edge[-1] + size)
    zed = [0] + [e + 1 for e in edge[1:-1]] + [NB]
    return edge, zed


def slots(piece):
    sizes = PIECES[piece][2]
    _, zed = bounds(sizes)
    return max(*sizes, *(b - a for a, b in zip(zed, zed[1:])))


def pad(out, used):
    for i in range(used, out.shape[0]):
        out[i] = jnp.zeros(out.shape[1:], out.dtype)


def gather_z(order, x0, out, piece, k):
    r0, rows, sizes = PIECES[piece]
    _, zed = bounds(sizes)
    for q in range(zed[k], zed[k + 1]):
        out[q - zed[k]] = x0[order[SRC, q], pl.ds(r0, rows), :]
    pad(out, zed[k + 1] - zed[k])


def head_kernel(first, pm_hbm, x_hbm, walk, x0, *rest):
    zouts, (pm, seen, sem) = rest[: len(first)], rest[len(first):]
    maps = pltpu.make_async_copy(pm_hbm, pm, sem.at[0])
    data = pltpu.make_async_copy(x_hbm, x0, sem.at[1])
    maps.start()
    data.start()
    for i in range(NB):
        seen[i] = 0
    maps.wait()

    def step(p, carry):
        cur, start, begin, scan = carry
        walk[CYC, p] = cur
        walk[ST, p] = begin
        seen[cur] = 1
        nxt = pm[1, cur]
        closes = nxt == start
        walk[NXT, p] = jnp.where(closes, begin, p + 1)

        def find():
            return lax.while_loop(
                lambda s: jnp.logical_and(s < NB - 1, seen[s] == 1), lambda s: s + 1, scan
            )

        scan = lax.cond(closes, find, lambda: scan)
        cur = jnp.where(closes, scan, nxt)
        start = jnp.where(closes, scan, start)
        begin = jnp.where(closes, p + 1, begin)
        return cur, start, begin, scan

    zero = jnp.int32(0)
    lax.fori_loop(0, NB, step, (zero, zero, zero, zero))
    data.wait()
    for (piece, k), out in zip(first, zouts):
        r0, rows, sizes = PIECES[piece]
        _, zed = bounds(sizes)
        for q in range(zed[k], zed[k + 1]):
            out[q - zed[k]] = x0[pm[0, walk[CYC, q]], pl.ds(r0, rows), :]
        pad(out, zed[k + 1] - zed[k])


def load_copies(level, d_ref, o_ref, w_ref, sem):
    return [
        pltpu.make_async_copy(ref.at[level], w_ref.at[half], sem.at[half])
        for half, ref in enumerate((d_ref, o_ref))
    ]


def tables_kernel(pm, walk, d_ref, o_ref, order, *refs):
    w_refs, (inv, sem) = refs[:4], refs[4:]
    copies = []
    for level in range(4):
        copies += load_copies(level, d_ref, o_ref, w_refs[level], sem.at[level])
    for copy in copies:
        copy.start()

    def invert(i, _):
        inv[pm[2, i]] = i
        return 0

    lax.fori_loop(0, NB, invert, 0, unroll=8)

    def fill(p, _):
        c = walk[CYC, p]
        order[CYC, p] = c
        order[SRC, p] = pm[0, c]
        order[NXT, p] = walk[NXT, p]
        order[ST, p] = walk[ST, p]
        order[TJ, p] = inv[c]
        order[POS, c] = p
        order[PM3, p] = pm[3, p]
        return 0

    lax.fori_loop(0, NB, fill, 0, unroll=8)
    for copy in copies:
        copy.wait()


def factors(w, j):
    return cat(w[0, j], w[1, j])


def level0_kernel(piece, k, after, *refs):
    refs = list(refs)
    order, x0, zin, w = refs[:4]
    del refs[:4]
    before = refs.pop(0) if k else None
    xs, msg = refs[:2]
    r0, rows, sizes = PIECES[piece]
    edge, zed = bounds(sizes)
    lo, count = edge[k], sizes[k]
    if k:
        xs[0] = before[sizes[k - 1]]
        begin = order[ST, lo]
        xs[count + 1] = before[jnp.where(begin >= edge[k - 1], begin - edge[k - 1], sizes[k - 1] + 1)]
    for q in range(zed[k], zed[k + 1]):
        c = order[CYC, q]
        mixed = mm(cat(x0[c, pl.ds(r0, rows), :], zin[q - zed[k]]), factors(w, c))
        xs[q - lo] = mixed.astype(BF)
    for i in range(count):
        nxt = order[NXT, lo + i]
        msg[i] = xs[jnp.where(nxt >= lo, nxt - lo, count + 1)]
    pad(msg, count)
    if after is not None:
        gather_z(order, x0, refs[2], *after)


def level1_kernel(piece, k, order, xs, yin, w, out):
    _, _, sizes = PIECES[piece]
    edge, _ = bounds(sizes)
    for i in range(sizes[k]):
        mixed = mm(cat(xs[i], yin[i]), factors(w, order[CYC, edge[k] + i]))
        out[i] = mixed.astype(BF)
    pad(out, sizes[k])


def early_kernel(piece, order, w, *refs):
    _, _, sizes = PIECES[piece]
    edge, _ = bounds(sizes)
    n = len(sizes)
    own, got, (x2, x3) = refs[:n], refs[n : 2 * n - 1], refs[2 * n - 1 :]
    for k in range(n):
        for i in range(sizes[k]):
            x2[edge[k] + i] = own[k][i]
    for k in range(n - 1):
        for i in range(sizes[k]):
            j = order[TJ, edge[k] + i]
            x3[edge[k] + i] = mm(cat(x2[order[POS, j]], got[k][i]), factors(w, j)).astype(BF)


def products(order, w3, full, quarter, out, base):
    q = NB // 4
    for i in range(q):
        j = quarter * q + i
        other = order[PM3, j]
        total = mm(cat(full[j], full[other]), cat(w3[0, j], w3[1, other]))
        out[base + i] = total.astype(out.dtype)


def near_far(order, w3, full, send, keep, far, near):
    me = lax.axis_index("hi")
    z, core = me // 2, me % 2
    base = 0
    for chip in ([1 - z] if far else []) + ([z] if near else []):
        products(order, w3, full, 2 * chip + 1 - core, send, base)
        products(order, w3, full, 2 * chip + core, keep, base)
        base += NB // 4


def late_kernel(piece, near, order, w, w3, x2, x3, got, send, keep, full):
    _, _, sizes = PIECES[piece]
    edge, _ = bounds(sizes)
    last = edge[-2]
    for i in range(last):
        full[order[TJ, i]] = x3[i]
    for i in range(sizes[-1]):
        j = order[TJ, last + i]
        full[j] = mm(cat(x2[order[POS, j]], got[i]), factors(w, j)).astype(BF)
    near_far(order, w3, full, send, keep, True, near)


def rest_kernel(order, w3, full, send, keep):
    near_far(order, w3, full, send, keep, False, True)


def join_kernel(keep, got, send, own=None):
    q = NB // 4
    send[...] = (keep[:q] + got[:q].astype(F32)).astype(BF)
    if own is not None:
        own[...] = (keep[q:] + got[q:].astype(F32))


def final_kernel(*refs):
    out = refs[-1]
    for piece, (r0, rows, _) in enumerate(PIECES):
        if piece < len(PIECES) - 1:
            own = refs[2 * piece][...]
            far = refs[2 * piece + 1]
        else:
            own = refs[2 * piece][...] + refs[2 * piece + 1][...].astype(F32)
            far = refs[2 * piece + 2]
        out[:, pl.ds(r0, rows), :] = (own + far[...].astype(F32)).astype(BF)


def plan():
    chunks = [(p, k) for p in range(len(PIECES)) for k in range(len(PIECES[p][2]))]
    count = len(chunks)
    steps = []
    for s in range(count):
        steps.append(("level0", *chunks[s]))
        if s:
            steps.append(("level1", *chunks[s - 1]))
    last = steps.pop()
    steps += [("early", 0, 0), last, ("late", 0, 0), ("level1", *chunks[-1])]
    steps += [("early", 1, 0), ("join", 0, 0), ("late", 1, 0), ("rest", 1, 0), ("join", 1, 0)]
    return chunks, steps


def body(blocks, diag, off, maps):
    hbm = lambda a: pltpu.with_memory_space_constraint(a, pltpu.HBM)
    blocks, diag, off = hbm(blocks), hbm(diag), hbm(off)
    chunks, steps = plan()

    def zshape(piece, k):
        return pltpu.VMEM((slots(piece), PIECES[piece][1], P_), BF)

    first = chunks[: DEPTH + 1]
    walk, x0, *zmsg = call(
        functools.partial(head_kernel, first),
        "head",
        [jax.ShapeDtypeStruct((3, NB), jnp.int32), pltpu.VMEM((NB, P_, P_), BF)]
        + [zshape(*c) for c in first],
        [hbm(maps), blocks],
        [ANY, ANY],
        (),
        scratch=[pltpu.SMEM((4, NB), jnp.int32), pltpu.SMEM((NB,), jnp.int32), pltpu.SemaphoreType.DMA((2,))],
        out_specs=[SM] + [VM] * (1 + len(first)),
    )
    zin = {c: partner_2(m, "lo", 0) for c, m in zip(first, zmsg)}
    wshape = pltpu.VMEM((2, NB, P_, P_), BF)
    order, *w = call(
        tables_kernel,
        "tables",
        [jax.ShapeDtypeStruct((8, NB), jnp.int32)] + [wshape] * 4,
        [maps, walk, diag, off],
        [SM, SM, ANY, ANY],
        (x0,),
        scratch=[pltpu.SMEM((NB,), jnp.int32), pltpu.SemaphoreType.DMA((4, 2))],
        out_specs=[SM] + [VM] * 4,
    )
    dep = x0
    top = lax.axis_size("lo").bit_length() - 1
    xs, yin, x2, xin, early, late, core, chip = {}, {}, {}, {}, {}, {}, {}, {}
    for kind, piece, k in steps:
        _, rows, sizes = PIECES[piece]
        c = (piece, k)
        name = f"{kind}_{piece}_{k}"
        dep = (dep, *w)
        part = lambda count, dtype: pltpu.VMEM((count, rows, P_), dtype)
        if kind == "level0":
            s = chunks.index(c)
            after = chunks[s + DEPTH] if 0 < s < len(chunks) - DEPTH else None
            outs = [part(sizes[k] + 2, BF), part(slots(piece), BF)]
            outs += [zshape(*after)] if after else []
            ins = [order, x0, zin[c], w[0]] + ([xs[piece, k - 1]] if k else [])
            specs = [SM] + [VM] * (len(ins) - 1)
            xs[c], msg, *more = call(
                functools.partial(level0_kernel, piece, k, after),
                name, outs, ins, specs, dep,
            )
            yin[c] = partner_2(msg, "lo", 1)
            if after:
                zin[after] = partner_2(more[0], "lo", 0)
            dep = xs[c]
        elif kind == "level1":
            s = chunks.index(c) - 2
            if s >= 0:
                dep = (*dep, xin[chunks[s]])
            (x2[c],) = call(
                functools.partial(level1_kernel, piece, k),
                name, [part(slots(piece), BF)],
                [order, xs[c], yin[c], w[1]], [SM, VM, VM, VM], dep,
            )
            xin[c] = partner_2(x2[c], "lo", top - 1)
            dep = x2[c]
        elif kind == "early":
            n = len(sizes)
            ins = [order, w[2]] + [x2[piece, i] for i in range(n)] + [xin[piece, i] for i in range(n - 1)]
            early[piece] = call(
                functools.partial(early_kernel, piece),
                name, [part(NB, BF), part(NB - sizes[-1], BF)],
                ins, [SM] + [VM] * (len(ins) - 1), dep, cost=20000000 if piece else 2000000,
            )
            dep = early[piece][0]
        elif kind == "late":
            split = piece == len(PIECES) - 1
            count = NB // 4 if split else NB // 2
            send, keep, full = call(
                functools.partial(late_kernel, piece, not split),
                name, [part(count, BF), part(count, F32), part(NB, BF)],
                [order, w[2], w[3], *early[piece], xin[piece, len(sizes) - 1]], [SM] + [VM] * 5, dep,
            )
            late[piece] = full
            core[piece] = keep, partner_2(send, "hi", 0)
            dep = keep
        elif kind == "rest":
            if piece:
                dep = (*dep, chip[piece - 1][1])
            send, keep = call(
                rest_kernel,
                name, [part(NB // 4, BF), part(NB // 4, F32)],
                [order, w[3], late[piece]], [SM, VM, VM], dep,
            )
            chip[piece] = keep, partner_2(send, "hi", 0)
            dep = keep
        else:
            split = piece == len(PIECES) - 1
            outs = [part(NB // 4, BF)] + ([] if split else [part(NB // 4, F32)])
            send, *own = call(join_kernel, name, outs, [*core[piece]], [VM, VM], dep)
            chip[piece] = *(chip[piece] if split else own), partner_2(send, "hi", 1)
            dep = send
    ins = [a for piece in range(len(PIECES)) for a in chip[piece]]
    (out,) = call(
        final_kernel, "final", [jax.ShapeDtypeStruct((NB // 4, P_, P_), BF)],
        ins, [VM] * len(ins), (),
    )
    return out


def solution(mesh):
    in_specs = (
        P(("hi", "lo"), None, None),
        P(None, ("hi", "lo"), None, None),
        P(None, ("hi", "lo"), None, None),
        P(),
    )
    out_specs = P(("lo", "hi"), None, None)
    return jax.shard_map(body, mesh=mesh, in_specs=in_specs, out_specs=out_specs, check_vma=False)
```

```python
import functools

import jax
import jax.numpy as jnp
from jax import lax
from jax.experimental import pallas as pl
from jax.experimental.pallas import tpu as pltpu
from jax.sharding import PartitionSpec as P

BF = jnp.bfloat16
F32 = jnp.float32
VM = pl.BlockSpec(memory_space=pltpu.VMEM)
SM = pl.BlockSpec(memory_space=pltpu.SMEM)
ANY = pl.BlockSpec(memory_space=pl.ANY)
NB = 64
P_ = 128
PIECES = ((0, 64, (21, 22, 21)), (64, 64, (21, 22, 21)))
DEPTH = 2
CYC, NXT, ST, SRC, TJ, POS, PM3 = range(7)


def partner_2(array, axis, apart):
    return lax.ppermute(array, axis, [(i, i ^ 1 << apart) for i in range(lax.axis_size(axis))])


def mm(left, right):
    return lax.dot_general(left, right, (((1,), (1,)), ((), ())), preferred_element_type=F32)


def cat(a, b):
    return jnp.concatenate([a, b], axis=1)


def call(kernel, name, outs, ins, specs, dep, scratch=(), mb=4, out_specs=None, cost=2000000):
    outs = tuple(outs)
    extra = tuple(dep)

    def run(*refs):
        refs = list(refs)
        n = len(ins)
        del refs[n : n + len(extra)]
        kernel(*refs)

    return pl.pallas_call(
        run,
        out_shape=outs,
        in_specs=list(specs) + [ANY] * len(extra),
        out_specs=tuple(out_specs or [VM] * len(outs)),
        scratch_shapes=list(scratch),
        compiler_params=pltpu.CompilerParams(vmem_limit_bytes=mb << 20),
        cost_estimate=pl.CostEstimate(flops=0, bytes_accessed=cost, transcendentals=0),
        name=name,
    )(*ins, *extra)


def bounds(sizes):
    edge = [0]
    for size in sizes:
        edge.append(edge[-1] + size)
    zed = [0] + [e + 1 for e in edge[1:-1]] + [NB]
    return edge, zed


def slots(piece):
    sizes = PIECES[piece][2]
    _, zed = bounds(sizes)
    return max(*sizes, *(b - a for a, b in zip(zed, zed[1:])))


def pad(out, used):
    return
    for i in range(used, out.shape[0]):
        out[i] = jnp.zeros(out.shape[1:], out.dtype)


def gather_z(order, x0, out, piece, k):
    r0, rows, sizes = PIECES[piece]
    _, zed = bounds(sizes)
    for q in range(zed[k], zed[k + 1]):
        out[q - zed[k]] = x0[order[SRC, q], pl.ds(r0, rows), :]
    pad(out, zed[k + 1] - zed[k])


def walk_cycles(pm, seen, walk, count):
    for i in range(NB):
        seen[i] = 0

    def step(p, carry):
        cur, start, begin, scan = carry
        walk[CYC, p] = cur
        walk[ST, p] = begin
        seen[cur] = 1
        nxt = pm[1, cur]
        closes = nxt == start
        walk[NXT, p] = jnp.where(closes, begin, p + 1)

        def find():
            return lax.while_loop(
                lambda s: jnp.logical_and(s < NB - 1, seen[s] == 1), lambda s: s + 1, scan
            )

        scan = lax.cond(closes, find, lambda: scan)
        cur = jnp.where(closes, scan, nxt)
        start = jnp.where(closes, scan, start)
        begin = jnp.where(closes, p + 1, begin)
        return cur, start, begin, scan

    zero = jnp.int32(0)
    lax.fori_loop(0, count, step, (zero, zero, zero, zero))


def gather_first(pm, walk, x0, out, piece, k):
    r0, rows, sizes = PIECES[piece]
    _, zed = bounds(sizes)
    for q in range(zed[k], zed[k + 1]):
        out[q - zed[k]] = x0[pm[0, walk[CYC, q]], pl.ds(r0, rows), :]
    pad(out, zed[k + 1] - zed[k])


def head_kernel(pm_hbm, x_hbm, pm, x0, out, walk, seen, sem):
    maps = pltpu.make_async_copy(pm_hbm, pm, sem.at[0])
    data = pltpu.make_async_copy(x_hbm, x0, sem.at[1])
    maps.start()
    data.start()
    maps.wait()
    walk_cycles(pm, seen, walk, bounds(PIECES[0][2])[1][1])
    data.wait()
    gather_first(pm, walk, x0, out, 0, 0)


def next_kernel(chunks, pm, x0, d_ref, o_ref, walk, w_ref, *rest):
    outs, (seen, sem) = rest[: len(chunks)], rest[len(chunks):]
    copies = load_copies(0, d_ref, o_ref, w_ref, sem)
    for copy in copies:
        copy.start()
    walk_cycles(pm, seen, walk, NB)
    for (piece, k), out in zip(chunks, outs):
        gather_first(pm, walk, x0, out, piece, k)
    for copy in copies:
        copy.wait()


def load_copies(level, d_ref, o_ref, w_ref, sem):
    return [
        pltpu.make_async_copy(ref.at[level], w_ref.at[half], sem.at[half])
        for half, ref in enumerate((d_ref, o_ref))
    ]


def tables_kernel(pm, walk, d_ref, o_ref, order, *refs):
    w_refs, (inv, sem) = refs[:-2], refs[-2:]
    copies = []
    for i, w_ref in enumerate(w_refs):
        copies += load_copies(i + 1, d_ref, o_ref, w_ref, sem.at[i])
    for copy in copies:
        copy.start()

    def invert(i, _):
        inv[pm[2, i]] = i
        return 0

    lax.fori_loop(0, NB, invert, 0, unroll=8)

    def fill(p, _):
        c = walk[CYC, p]
        order[CYC, p] = c
        order[SRC, p] = pm[0, c]
        order[NXT, p] = walk[NXT, p]
        order[ST, p] = walk[ST, p]
        order[TJ, p] = inv[c]
        order[POS, c] = p
        order[PM3, p] = pm[3, p]
        return 0

    lax.fori_loop(0, NB, fill, 0, unroll=8)
    for copy in copies:
        copy.wait()


def factors(w, j):
    return cat(w[0, j], w[1, j])


def level0_kernel(piece, k, after, *refs):
    refs = list(refs)
    order, x0, zin, w = refs[:4]
    del refs[:4]
    before = refs.pop(0) if k else None
    xs, msg = refs[:2]
    r0, rows, sizes = PIECES[piece]
    edge, zed = bounds(sizes)
    lo, count = edge[k], sizes[k]
    if k:
        xs[0] = before[sizes[k - 1]]
        begin = order[ST, lo]
        xs[count + 1] = before[jnp.where(begin >= edge[k - 1], begin - edge[k - 1], sizes[k - 1] + 1)]
    for q in range(zed[k], zed[k + 1]):
        c = order[CYC, q]
        mixed = mm(cat(x0[c, pl.ds(r0, rows), :], zin[q - zed[k]]), factors(w, c))
        xs[q - lo] = mixed.astype(BF)
    for i in range(count):
        nxt = order[NXT, lo + i]
        msg[i] = xs[jnp.where(nxt >= lo, nxt - lo, count + 1)]
    pad(msg, count)
    if after is not None:
        gather_z(order, x0, refs[2], *after)


def level1_kernel(piece, k, order, xs, yin, w, out):
    _, _, sizes = PIECES[piece]
    edge, _ = bounds(sizes)
    for i in range(sizes[k]):
        mixed = mm(cat(xs[i], yin[i]), factors(w, order[CYC, edge[k] + i]))
        out[i] = mixed.astype(BF)
    pad(out, sizes[k])


def early_kernel(piece, order, w, *refs):
    _, _, sizes = PIECES[piece]
    edge, _ = bounds(sizes)
    n = len(sizes)
    own, got, (x2, x3) = refs[:n], refs[n : 2 * n - 1], refs[2 * n - 1 :]
    for k in range(n):
        for i in range(sizes[k]):
            x2[edge[k] + i] = own[k][i]
    for k in range(n - 1):
        for i in range(sizes[k]):
            j = order[TJ, edge[k] + i]
            x3[edge[k] + i] = mm(cat(x2[order[POS, j]], got[k][i]), factors(w, j)).astype(BF)


def products(order, w3, full, quarters, outs):
    q = NB // 4
    for quarter, out in zip(quarters, outs):
        for i in range(q):
            j = quarter * q + i
            other = order[PM3, j]
            total = mm(cat(full[j], full[other]), cat(w3[0, j], w3[1, other]))
            ref = out[i // out[0].shape[0]]
            ref[i % out[0].shape[0]] = total.astype(ref.dtype)


def late_kernel(piece, order, w, w3, x2, x3, got, send, keep, full):
    _, _, sizes = PIECES[piece]
    edge, _ = bounds(sizes)
    last = edge[-2]
    for i in range(last):
        full[order[TJ, i]] = x3[i]
    for i in range(sizes[-1]):
        j = order[TJ, last + i]
        full[j] = mm(cat(x2[order[POS, j]], got[i]), factors(w, j)).astype(BF)
    me = lax.axis_index("hi")
    z, core = me // 2, me % 2
    products(order, w3, full, (2 * (1 - z) + 1 - core, 2 * (1 - z) + core), ([send], [keep]))


def rest_kernel(order, w3, full, *outs):
    *sends, keep = outs
    me = lax.axis_index("hi")
    z, core = me // 2, me % 2
    products(order, w3, full, (2 * z + 1 - core, 2 * z + core), (sends, [keep]))


def join_kernel(keep, got, send):
    send[...] = (keep[...] + got[...].astype(F32)).astype(BF)


def final_kernel(*refs):
    refs, out = list(refs[:-1]), refs[-1]
    for piece, (r0, rows, _) in enumerate(PIECES):
        far, own, *cores = refs[: 3 + piece]
        del refs[: 3 + piece]
        base = 0
        for core in cores:
            part = pl.ds(base, core.shape[0])
            base += core.shape[0]
            total = own[part] + core[...].astype(F32) + far[part].astype(F32)
            out[part, pl.ds(r0, rows), :] = total.astype(BF)


def plan():
    chunks = [(p, k) for p in range(len(PIECES)) for k in range(len(PIECES[p][2]))]
    count = len(chunks)
    steps = []
    for s in range(count):
        steps.append(("level0", *chunks[s]))
        if s:
            steps.append(("level1", *chunks[s - 1]))
    last = steps.pop()
    steps += [last, ("early", 0, 0), ("late", 0, 0), ("rest", 0, 0), ("level1", *chunks[-1])]
    steps += [("early", 1, 0), ("join", 0, 0), ("late", 1, 0), ("join", 1, 0), ("rest", 1, 0)]
    return chunks, steps


def body(blocks, diag, off, maps):
    hbm = lambda a: pltpu.with_memory_space_constraint(a, pltpu.HBM)
    blocks, diag, off = hbm(blocks), hbm(diag), hbm(off)
    chunks, steps = plan()

    def zshape(piece, k):
        _, zed = bounds(PIECES[piece][2])
        return pltpu.VMEM((zed[k + 1] - zed[k], PIECES[piece][1], P_), BF)

    first = chunks[: DEPTH + 1]
    wshape = pltpu.VMEM((2, NB, P_, P_), BF)
    pm, x0, zmsg = call(
        head_kernel,
        "head",
        [pltpu.SMEM((4, NB), jnp.int32), pltpu.VMEM((NB, P_, P_), BF), zshape(*first[0])],
        [hbm(maps), blocks],
        [ANY, ANY],
        (),
        scratch=[pltpu.SMEM((3, NB), jnp.int32), pltpu.SMEM((NB,), jnp.int32), pltpu.SemaphoreType.DMA((2,))],
        out_specs=[SM, VM, VM],
    )
    walk, w0, *more = call(
        functools.partial(next_kernel, first[1:]),
        "next",
        [pltpu.SMEM((3, NB), jnp.int32), wshape] + [zshape(*c) for c in first[1:]],
        [pm, x0, diag, off],
        [SM, VM, ANY, ANY],
        (),
        scratch=[pltpu.SMEM((NB,), jnp.int32), pltpu.SemaphoreType.DMA((2,))],
        out_specs=[SM] + [VM] * len(first),
    )
    zmsg = [zmsg] + more
    zin = {c: partner_2(m, "lo", 0) for c, m in zip(first, zmsg)}
    order, *w = call(
        tables_kernel,
        "tables",
        [pltpu.SMEM((8, NB), jnp.int32)] + [wshape] * 3,
        [pm, walk, diag, off],
        [SM, SM, ANY, ANY],
        (w0,),
        scratch=[pltpu.SMEM((NB,), jnp.int32), pltpu.SemaphoreType.DMA((3, 2))],
        out_specs=[SM] + [VM] * 3,
    )
    w = [w0, *w]
    dep = x0
    top = lax.axis_size("lo").bit_length() - 1
    xs, yin, x2, xin, early, late, core, chip, far = {}, {}, {}, {}, {}, {}, {}, {}, {}
    for kind, piece, k in steps:
        _, rows, sizes = PIECES[piece]
        c = (piece, k)
        name = f"{kind}_{piece}_{k}"
        dep = (dep, *w)
        part = lambda count, dtype: pltpu.VMEM((count, rows, P_), dtype)
        if kind == "level0":
            s = chunks.index(c)
            if s > 2:
                dep = (*dep, xin[chunks[s - 3]])
            after = chunks[s + DEPTH] if 0 < s < len(chunks) - DEPTH else None
            outs = [part(sizes[k] + 2, BF), part(sizes[k], BF)]
            outs += [zshape(*after)] if after else []
            ins = [order, x0, zin[c], w[0]] + ([xs[piece, k - 1]] if k else [])
            specs = [SM] + [VM] * (len(ins) - 1)
            xs[c], msg, *more = call(
                functools.partial(level0_kernel, piece, k, after),
                name, outs, ins, specs, dep,
            )
            yin[c] = partner_2(msg, "lo", 1)
            if after:
                zin[after] = partner_2(more[0], "lo", 0)
            dep = xs[c]
        elif kind == "level1":
            (x2[c],) = call(
                functools.partial(level1_kernel, piece, k),
                name, [part(sizes[k], BF)],
                [order, xs[c], yin[c], w[1]], [SM, VM, VM, VM], dep,
            )
            xin[c] = partner_2(x2[c], "lo", top - 1)
            dep = x2[c]
        elif kind == "early":
            n = len(sizes)
            ins = [order, w[2]] + [x2[piece, i] for i in range(n)] + [xin[piece, i] for i in range(n - 1)]
            early[piece] = call(
                functools.partial(early_kernel, piece),
                name, [part(NB, BF), part(NB - sizes[-1], BF)],
                ins, [SM] + [VM] * (len(ins) - 1), dep, cost=20000000 if piece else 2000000,
            )
            dep = early[piece][0]
        elif kind == "late":
            if piece:
                dep = (*dep, *chip[piece - 1][1:])
            send, keep, full = call(
                functools.partial(late_kernel, piece),
                name, [part(NB // 4, BF), part(NB // 4, F32), part(NB, BF)],
                [order, w[2], w[3], *early[piece], xin[piece, len(sizes) - 1]], [SM] + [VM] * 5, dep,
            )
            late[piece] = full
            core[piece] = keep, partner_2(send, "hi", 0)
            dep = keep
        elif kind == "rest":
            if not piece:
                dep = (*dep, xin[chunks[-3]])
            count = 1 + piece
            *sends, keep = call(
                rest_kernel,
                name, [part(NB // 4 // count, BF)] * count + [part(NB // 4, F32)],
                [order, w[3], late[piece]], [SM, VM, VM], dep,
            )
            chip[piece] = keep, *[partner_2(send, "hi", 0) for send in sends]
            dep = keep
        else:
            if piece:
                dep = (*dep, far[piece - 1])
            (send,) = call(join_kernel, name, [part(NB // 4, BF)], [*core[piece]], [VM, VM], dep)
            far[piece] = partner_2(send, "hi", 1)
            dep = send
    ins = [a for piece in range(len(PIECES)) for a in (far[piece], *chip[piece])]
    (out,) = call(
        final_kernel, "final", [jax.ShapeDtypeStruct((NB // 4, P_, P_), BF)],
        ins, [VM] * len(ins), (),
    )
    return out


def solution(mesh):
    in_specs = (
        P(("hi", "lo"), None, None),
        P(None, ("hi", "lo"), None, None),
        P(None, ("hi", "lo"), None, None),
        P(),
    )
    out_specs = P(("lo", "hi"), None, None)
    return jax.shard_map(body, mesh=mesh, in_specs=in_specs, out_specs=out_specs, check_vma=False)
```

```python
import functools

import jax
import jax.numpy as jnp
from jax import lax
from jax.experimental import pallas as pl
from jax.experimental.pallas import tpu as pltpu
from jax.sharding import PartitionSpec as P

BF = jnp.bfloat16
F32 = jnp.float32
VM = pl.BlockSpec(memory_space=pltpu.VMEM)
SM = pl.BlockSpec(memory_space=pltpu.SMEM)
ANY = pl.BlockSpec(memory_space=pl.ANY)
NB = 64
P_ = 128
PIECES = ((0, 64, (21, 22, 21)), (64, 64, (21, 22, 21)))
DEPTH = 2
CYC, NXT, ST, SRC, TJ, POS, PM3 = range(7)


def partner_2(array, axis, apart):
    return lax.ppermute(array, axis, [(i, i ^ 1 << apart) for i in range(lax.axis_size(axis))])


def mm(left, right):
    return lax.dot_general(left, right, (((1,), (1,)), ((), ())), preferred_element_type=F32)


def cat(a, b):
    return jnp.concatenate([a, b], axis=1)


def call(kernel, name, outs, ins, specs, dep, scratch=(), mb=4, out_specs=None, cost=2000000, aliases=None):
    outs = tuple(outs)
    extra = tuple(dep)

    def run(*refs):
        refs = list(refs)
        n = len(ins)
        del refs[n : n + len(extra)]
        kernel(*refs)

    return pl.pallas_call(
        run,
        out_shape=outs,
        in_specs=list(specs) + [ANY] * len(extra),
        out_specs=tuple(out_specs or [VM] * len(outs)),
        scratch_shapes=list(scratch),
        compiler_params=pltpu.CompilerParams(vmem_limit_bytes=mb << 20),
        cost_estimate=pl.CostEstimate(flops=0, bytes_accessed=cost, transcendentals=0),
        name=name,
        input_output_aliases=aliases or {},
    )(*ins, *extra)


def bounds(sizes):
    edge = [0]
    for size in sizes:
        edge.append(edge[-1] + size)
    zed = [0] + [e + 1 for e in edge[1:-1]] + [NB]
    return edge, zed


def slots(piece):
    sizes = PIECES[piece][2]
    _, zed = bounds(sizes)
    return max(*sizes, *(b - a for a, b in zip(zed, zed[1:])))


def pad(out, used):
    for i in range(used, out.shape[0]):
        out[i] = jnp.zeros(out.shape[1:], out.dtype)


def gather_z(order, x0, out, piece, k):
    r0, rows, sizes = PIECES[piece]
    _, zed = bounds(sizes)
    for q in range(zed[k], zed[k + 1]):
        out[q - zed[k]] = x0[order[SRC, q], pl.ds(r0, rows), :]
    pad(out, zed[k + 1] - zed[k])


def walk_cycles(pm, seen, walk, count):
    for i in range(NB):
        seen[i] = 0

    def step(p, carry):
        cur, start, begin, scan = carry
        walk[CYC, p] = cur
        walk[ST, p] = begin
        seen[cur] = 1
        nxt = pm[1, cur]
        closes = nxt == start
        walk[NXT, p] = jnp.where(closes, begin, p + 1)

        def find():
            return lax.while_loop(
                lambda s: jnp.logical_and(s < NB - 1, seen[s] == 1), lambda s: s + 1, scan
            )

        scan = lax.cond(closes, find, lambda: scan)
        cur = jnp.where(closes, scan, nxt)
        start = jnp.where(closes, scan, start)
        begin = jnp.where(closes, p + 1, begin)
        return cur, start, begin, scan

    zero = jnp.int32(0)
    lax.fori_loop(0, count, step, (zero, zero, zero, zero))


def gather_first(pm, walk, x0, out, piece, k):
    r0, rows, sizes = PIECES[piece]
    _, zed = bounds(sizes)
    for q in range(zed[k], zed[k + 1]):
        out[q - zed[k]] = x0[pm[0, walk[CYC, q]], pl.ds(r0, rows), :]
    pad(out, zed[k + 1] - zed[k])


def head_kernel(pm_hbm, x_hbm, pm, x0, out, walk, seen, sem):
    maps = pltpu.make_async_copy(pm_hbm, pm, sem.at[0])
    data = pltpu.make_async_copy(x_hbm, x0, sem.at[1])
    maps.start()
    data.start()
    maps.wait()
    walk_cycles(pm, seen, walk, bounds(PIECES[0][2])[1][1])
    data.wait()
    gather_first(pm, walk, x0, out, 0, 0)


def next_kernel(chunks, pm, x0, d_ref, o_ref, walk, w_ref, *rest):
    outs, (seen, sem) = rest[: len(chunks)], rest[len(chunks):]
    copies = load_copies(0, d_ref, o_ref, w_ref, sem)
    for copy in copies:
        copy.start()
    walk_cycles(pm, seen, walk, NB)
    for (piece, k), out in zip(chunks, outs):
        gather_first(pm, walk, x0, out, piece, k)
    for copy in copies:
        copy.wait()


def load_copies(level, d_ref, o_ref, w_ref, sem):
    return [
        pltpu.make_async_copy(ref.at[level], w_ref.at[half], sem.at[half])
        for half, ref in enumerate((d_ref, o_ref))
    ]


def tables_kernel(pm, walk, d_ref, o_ref, order, *refs):
    w_refs, (inv, sem) = refs[:-2], refs[-2:]
    copies = []
    for i, w_ref in enumerate(w_refs):
        copies += load_copies(i + 1, d_ref, o_ref, w_ref, sem.at[i])
    for copy in copies:
        copy.start()

    def invert(i, _):
        inv[pm[2, i]] = i
        return 0

    lax.fori_loop(0, NB, invert, 0, unroll=8)

    def fill(p, _):
        c = walk[CYC, p]
        order[CYC, p] = c
        order[SRC, p] = pm[0, c]
        order[NXT, p] = walk[NXT, p]
        order[ST, p] = walk[ST, p]
        order[TJ, p] = inv[c]
        order[POS, c] = p
        order[PM3, p] = pm[3, p]
        return 0

    lax.fori_loop(0, NB, fill, 0, unroll=8)
    for copy in copies:
        copy.wait()


def factors(w, j):
    return cat(w[0, j], w[1, j])


def level0_kernel(piece, k, after, *refs):
    refs = list(refs)
    order, x0, zin, w = refs[:4]
    del refs[:4]
    before = refs.pop(0) if k else None
    xs, msg = refs[:2]
    r0, rows, sizes = PIECES[piece]
    edge, zed = bounds(sizes)
    lo, count = edge[k], sizes[k]
    if k:
        xs[0] = before[sizes[k - 1]]
        begin = order[ST, lo]
        xs[count + 1] = before[jnp.where(begin >= edge[k - 1], begin - edge[k - 1], sizes[k - 1] + 1)]
    for q in range(zed[k], zed[k + 1]):
        c = order[CYC, q]
        mixed = mm(cat(x0[c, pl.ds(r0, rows), :], zin[q - zed[k]]), factors(w, c))
        xs[q - lo] = mixed.astype(BF)
    for i in range(count):
        nxt = order[NXT, lo + i]
        msg[i] = xs[jnp.where(nxt >= lo, nxt - lo, count + 1)]
    pad(msg, count)
    if after is not None:
        gather_z(order, x0, refs[2], *after)


def level1_kernel(piece, k, order, xs, yin, w, out):
    _, _, sizes = PIECES[piece]
    edge, _ = bounds(sizes)
    for i in range(sizes[k]):
        mixed = mm(cat(xs[i], yin[i]), factors(w, order[CYC, edge[k] + i]))
        out[i] = mixed.astype(BF)
    pad(out, sizes[k])


def early_kernel(piece, order, w, *refs):
    _, _, sizes = PIECES[piece]
    edge, _ = bounds(sizes)
    n = len(sizes)
    own, got, (x2, x3) = refs[:n], refs[n : 2 * n - 1], refs[2 * n - 1 :]
    for k in range(n):
        for i in range(sizes[k]):
            x2[edge[k] + i] = own[k][i]
    for k in range(n - 1):
        for i in range(sizes[k]):
            j = order[TJ, edge[k] + i]
            x3[edge[k] + i] = mm(cat(x2[order[POS, j]], got[k][i]), factors(w, j)).astype(BF)


def products(order, w3, full, quarters, outs):
    q = NB // 4
    for quarter, out in zip(quarters, outs):
        for i in range(q):
            j = quarter * q + i
            other = order[PM3, j]
            total = mm(cat(full[j], full[other]), cat(w3[0, j], w3[1, other]))
            ref = out[i // out[0].shape[0]]
            ref[i % out[0].shape[0]] = total.astype(ref.dtype)


def place():
    me = lax.axis_index("hi")
    return me // 2, me % 2


def late_kernel(piece, order, w, w3, x2, x3, got, *outs):
    send, keep, full = outs if len(outs) == 3 else (outs[0], None, outs[1])
    _, _, sizes = PIECES[piece]
    edge, _ = bounds(sizes)
    last = edge[-2]
    for i in range(last):
        full[order[TJ, i]] = x3[i]
    for i in range(sizes[-1]):
        j = order[TJ, last + i]
        full[j] = mm(cat(x2[order[POS, j]], got[i]), factors(w, j)).astype(BF)
    z, core = place()
    products(order, w3, full, [2 * (1 - z) + 1 - core], ([send],))
    if keep is not None:
        products(order, w3, full, [2 * (1 - z) + core], ([keep],))


def keep_kernel(order, w3, full, keep):
    z, core = place()
    products(order, w3, full, [2 * (1 - z) + core], ([keep],))


def rest_kernel(order, w3, full, *outs):
    *sends, keep = outs
    z, core = place()
    products(order, w3, full, (2 * z + 1 - core, 2 * z + core), (sends, [keep]))


def join_kernel(keep, got, send):
    send[...] = (keep[...] + got[...].astype(F32)).astype(BF)


def final_kernel(piece, *refs):
    r0, rows, _ = PIECES[piece]
    refs = list(refs)
    far, own, *cores = refs[: 3 + piece]
    out, stage, sem = refs[-3:]
    base, copies = 0, []
    for i, core in enumerate(cores):
        part = pl.ds(base, core.shape[0])
        base += core.shape[0]
        total = own[part] + core[...].astype(F32) + far[part].astype(F32)
        stage[part] = total.astype(BF)
        copies.append(
            pltpu.make_async_copy(stage.at[part], out.at[part, pl.ds(r0, rows), :], sem.at[i])
        )
        copies[-1].start()
    for copy in copies:
        copy.wait()


def plan():
    chunks = [(p, k) for p in range(len(PIECES)) for k in range(len(PIECES[p][2]))]
    count = len(chunks)
    steps = []
    for s in range(count):
        steps.append(("level0", *chunks[s]))
        if s:
            steps.append(("level1", *chunks[s - 1]))
    last = steps.pop()
    steps += [("early", 0, 0), last, ("late", 0, 0), ("rest", 0, 0), ("level1", *chunks[-1])]
    steps += [("early", 1, 0), ("join", 0, 0), ("late", 1, 0), ("join", 1, 0), ("rest", 1, 0)]
    steps += [("final", 0, 0), ("final", 1, 0)]
    return chunks, steps


def body(blocks, diag, off, maps):
    hbm = lambda a: pltpu.with_memory_space_constraint(a, pltpu.HBM)
    blocks, diag, off = hbm(blocks), hbm(diag), hbm(off)
    chunks, steps = plan()

    def zshape(piece, k):
        _, zed = bounds(PIECES[piece][2])
        size = zed[k + 1] - zed[k] if (piece, k) == chunks[-1] else slots(piece)
        return pltpu.VMEM((size, PIECES[piece][1], P_), BF)

    first = chunks[: DEPTH + 1]
    wshape = pltpu.VMEM((2, NB, P_, P_), BF)
    pm, x0, zmsg = call(
        head_kernel,
        "head",
        [pltpu.SMEM((4, NB), jnp.int32), pltpu.VMEM((NB, P_, P_), BF), zshape(*first[0])],
        [hbm(maps), blocks],
        [ANY, ANY],
        (),
        scratch=[pltpu.SMEM((3, NB), jnp.int32), pltpu.SMEM((NB,), jnp.int32), pltpu.SemaphoreType.DMA((2,))],
        out_specs=[SM, VM, VM],
    )
    walk, w0, *more = call(
        functools.partial(next_kernel, first[1:]),
        "next",
        [pltpu.SMEM((3, NB), jnp.int32), wshape] + [zshape(*c) for c in first[1:]],
        [pm, x0, diag, off],
        [SM, VM, ANY, ANY],
        (),
        scratch=[pltpu.SMEM((NB,), jnp.int32), pltpu.SemaphoreType.DMA((2,))],
        out_specs=[SM] + [VM] * len(first),
    )
    zmsg = [zmsg] + more
    zin = {c: partner_2(m, "lo", 0) for c, m in zip(first, zmsg)}
    order, *w = call(
        tables_kernel,
        "tables",
        [pltpu.SMEM((8, NB), jnp.int32)] + [wshape] * 3,
        [pm, walk, diag, off],
        [SM, SM, ANY, ANY],
        (w0,),
        scratch=[pltpu.SMEM((NB,), jnp.int32), pltpu.SemaphoreType.DMA((3, 2))],
        out_specs=[SM] + [VM] * 3,
    )
    w = [w0, *w]
    dep = x0
    top = lax.axis_size("lo").bit_length() - 1
    xs, yin, x2, xin, early, late, core, chip, far = {}, {}, {}, {}, {}, {}, {}, {}, {}
    for kind, piece, k in steps:
        _, rows, sizes = PIECES[piece]
        c = (piece, k)
        name = f"{kind}_{piece}_{k}"
        dep = (dep, *w)
        part = lambda count, dtype: pltpu.VMEM((count, rows, P_), dtype)
        if kind == "level0":
            s = chunks.index(c)
            if 2 < s < len(chunks) - 1:
                dep = (*dep, xin[chunks[s - 3]])
            after = chunks[s + DEPTH] if 0 < s < len(chunks) - DEPTH else None
            outs = [part(sizes[k] + 2, BF), part(sizes[k] if c == chunks[-1] else slots(piece), BF)]
            outs += [zshape(*after)] if after else []
            ins = [order, x0, zin[c], w[0]] + ([xs[piece, k - 1]] if k else [])
            specs = [SM] + [VM] * (len(ins) - 1)
            xs[c], msg, *more = call(
                functools.partial(level0_kernel, piece, k, after),
                name, outs, ins, specs, dep,
            )
            yin[c] = partner_2(msg, "lo", 1)
            if after:
                zin[after] = partner_2(more[0], "lo", 0)
            dep = xs[c]
        elif kind == "level1":
            (x2[c],) = call(
                functools.partial(level1_kernel, piece, k),
                name, [part(sizes[k] if c == chunks[-1] else slots(piece), BF)],
                [order, xs[c], yin[c], w[1]], [SM, VM, VM, VM], dep,
            )
            xin[c] = partner_2(x2[c], "lo", top - 1)
            dep = x2[c]
        elif kind == "early":
            n = len(sizes)
            if not piece:
                dep = (*dep, xin[chunks[-4]])
            ins = [order, w[2]] + [x2[piece, i] for i in range(n)] + [xin[piece, i] for i in range(n - 1)]
            early[piece] = call(
                functools.partial(early_kernel, piece),
                name, [part(NB, BF), part(NB - sizes[-1], BF)],
                ins, [SM] + [VM] * (len(ins) - 1), dep, cost=20000000 if piece else 2000000,
            )
            dep = early[piece][0]
        elif kind == "late":
            if piece:
                dep = (*dep, *chip[piece - 1][1:])
            outs = [part(NB // 4, BF), part(NB, BF)]
            send, *keep, full = call(
                functools.partial(late_kernel, piece),
                name, outs if piece else [outs[0], part(NB // 4, F32), outs[1]],
                [order, w[2], w[3], *early[piece], xin[piece, len(sizes) - 1]], [SM] + [VM] * 5, dep,
            )
            late[piece] = full
            got = partner_2(send, "hi", 0)
            dep = send
            if piece:
                keep = call(
                    keep_kernel, "keep", [part(NB // 4, F32)], [order, w[3], full], [SM, VM, VM], (dep, *w),
                )
                dep = keep[0]
            core[piece] = keep[0], got
        elif kind == "rest":
            if not piece:
                dep = (*dep, xin[chunks[-3]])
            count = 1 + piece
            *sends, keep = call(
                rest_kernel,
                name, [part(NB // 4 // count, BF)] * count + [part(NB // 4, F32)],
                [order, w[3], late[piece]], [SM, VM, VM], dep,
            )
            chip[piece] = keep, *[partner_2(send, "hi", 0) for send in sends]
            dep = keep
        elif kind == "final":
            ins = [far[piece], *chip[piece]] + ([out] if piece else [])
            (out,) = call(
                functools.partial(final_kernel, piece),
                name, [jax.ShapeDtypeStruct((NB // 4, P_, P_), BF)],
                ins, [VM] * (2 + 1 + piece) + ([ANY] if piece else []), () if piece else dep,
                scratch=[pltpu.VMEM((NB // 4, rows, P_), BF), pltpu.SemaphoreType.DMA((2,))],
                out_specs=[ANY], aliases={len(ins) - 1: 0} if piece else None,
            )
            dep = out
        else:
            if piece:
                dep = (*dep, far[piece - 1])
            (send,) = call(join_kernel, name, [part(NB // 4, BF)], [*core[piece]], [VM, VM], dep)
            far[piece] = partner_2(send, "hi", 1)
            dep = send
    return out


def solution(mesh):
    in_specs = (
        P(("hi", "lo"), None, None),
        P(None, ("hi", "lo"), None, None),
        P(None, ("hi", "lo"), None, None),
        P(),
    )
    out_specs = P(("lo", "hi"), None, None)
    return jax.shard_map(body, mesh=mesh, in_specs=in_specs, out_specs=out_specs, check_vma=False)
```
